32 devices in a mesh: lon: 16 (over z, y, core), lat: 2 (over x).
Axes of the slice: x: 2, y: 2, z: 4, core: 2. Of those that a mesh axis runs over, the one named last changes fastest.
Arguments:
- thermal_deviation: float32 [8, 128, 2048], P(None, 'lat', 'lon'), may hold values from -6 to 6
- saltiness_deviation: float32 [8, 128, 2048], P(None, 'lat', 'lon'), may hold values from -6 to 6
- zonal_current_speed: float32 [8, 128, 2048], P(None, 'lat', 'lon'), may hold values from -3 to 3
- meridional_flow_speed: float32 [8, 128, 2048], P(None, 'lat', 'lon'), may hold values from -3 to 3
- water_indicator: int32 [8, 128, 2048], P(None, 'lat', 'lon'), may hold values 0 or 1
Outputs:
- new_temperature: float32 [8, 128, 2048], P(None, 'lat', 'lon')
- new_salinity: float32 [8, 128, 2048], P(None, 'lat', 'lon')
- new_zonal: float32 [8, 128, 2048], P(None, 'lat', 'lon')
- new_meridional: float32 [8, 128, 2048], P(None, 'lat', 'lon')
The draws below stay inside these ranges and needn't reach their ends.
All inputs are finite; a program needn't handle non-finite values. No bound on the sum of `water_indicator` on one device may be relied on, other than what follows from the above.
Results may differ from the reference program's by a relative error of at most 0.00002.
Values sent between devices are 32-bit elements; how exact they have to be, the bound alone decides.
A program may use at most 64 MiB of HBM per device.

```python
import jax
import jax.numpy as jnp

VERTICAL_LAYERS = 8
STEPS = 4
PARALLEL_POINTS = 2048
MERIDIAN_POINTS = 128


def with_ends(values, rng, smallest, high):
    longest = values.shape.index(max(values.shape))
    spots = []
    for shift in (0, 1):
        where = [jax.random.randint(jax.random.fold_in(rng, axis), (), 0, length) for axis, length in enumerate(values.shape)]
        where[longest] = (where[longest] + shift) % values.shape[longest]
        spots.append(tuple(where))
    return values.at[spots[0]].set(smallest).at[spots[1]].set(high)


def block_levels(stream_key, dims, pieces, smallest, high):
    def one(dim, parts):
        draws = jax.random.uniform(jax.random.fold_in(jax.random.fold_in(stream_key, 6), dim), (parts,), jnp.float32, smallest / len(pieces), high / len(pieces))
        return jnp.repeat(jnp.exp(draws), dims[dim] // parts).reshape((-1,) + (1,) * (len(dims) - dim - 1))

    gain = one(*pieces[0])
    for cut in pieces[1:]:
        gain = gain * one(*cut)
    return gain


def gaussian(rng, shape, width, most, shards=(), kind=jnp.bfloat16):
    values = width * jax.random.normal(rng, shape, jnp.float32)
    if shards:
        values = values * block_levels(rng, shape, shards, -0.22, 0.18)
    return jnp.clip(values, -most, most).astype(kind)


def setup_inputs(seed: int = 0) -> dict:
    arg_keys = jax.random.split(jax.random.key(seed), 6)
    return {
        "thermal_deviation": gaussian(arg_keys[0], (VERTICAL_LAYERS, MERIDIAN_POINTS, PARALLEL_POINTS), 1.0, 6.0, ((1, 2), (2, 16)), jnp.float32),
        "saltiness_deviation": gaussian(arg_keys[1], (VERTICAL_LAYERS, MERIDIAN_POINTS, PARALLEL_POINTS), 1.0, 6.0, ((1, 2), (2, 16)), jnp.float32),
        "zonal_current_speed": gaussian(arg_keys[2], (VERTICAL_LAYERS, MERIDIAN_POINTS, PARALLEL_POINTS), 0.5, 3.0, ((1, 2), (2, 16)), jnp.float32),
        "meridional_flow_speed": gaussian(arg_keys[3], (VERTICAL_LAYERS, MERIDIAN_POINTS, PARALLEL_POINTS), 0.5, 3.0, ((1, 2), (2, 16)), jnp.float32),
        "water_indicator": with_ends((jax.random.randint(arg_keys[4], (VERTICAL_LAYERS, MERIDIAN_POINTS, PARALLEL_POINTS), 0, 4) < 3).astype(jnp.int32), jax.random.fold_in(arg_keys[4], 1), 0, 1),
    }


DIFFUSION = 0.1
HYPERDIFF = 0.01
ADVECTION = 0.25
EXPANSION = 0.2
CONTRACTION = 0.15
PRESSURE_COEF = 0.05
CORIOLIS_MAX = 0.3


def laplace(field, wet):
    centre = field[..., 1:-1, 1:-1]
    total = wet[..., 1:-1, 2:] * (field[..., 1:-1, 2:] - centre)
    total = total + wet[..., 1:-1, :-2] * (field[..., 1:-1, :-2] - centre)
    total = total + wet[..., 2:, 1:-1] * (field[..., 2:, 1:-1] - centre)
    total = total + wet[..., :-2, 1:-1] * (field[..., :-2, 1:-1] - centre)
    return total


def slope_x(field, wet):
    centre = field[..., 2:-2, 2:-2]
    east = wet[..., 2:-2, 3:-1] * (field[..., 2:-2, 3:-1] - centre)
    west = wet[..., 2:-2, 1:-3] * (field[..., 2:-2, 1:-3] - centre)
    return 0.5 * (east - west)


def slope_y(field, wet):
    centre = field[..., 2:-2, 2:-2]
    north = wet[..., 3:-1, 2:-2] * (field[..., 3:-1, 2:-2] - centre)
    south = wet[..., 1:-3, 2:-2] * (field[..., 1:-3, 2:-2] - centre)
    return 0.5 * (north - south)


def advance(extended, mask_ext, coriolis):
    first_lap = laplace(extended, mask_ext)
    second_lap = laplace(first_lap, mask_ext[:, 1:-1, 1:-1])
    inner_lap = first_lap[..., 1:-1, 1:-1]
    centre = extended[..., 2:-2, 2:-2]
    mask_centre = mask_ext[:, 2:-2, 2:-2]
    grad_east = slope_x(extended, mask_ext)
    grad_north = slope_y(extended, mask_ext)
    zonal = centre[2]
    merid = centre[3]
    density = CONTRACTION * extended[1] - EXPANSION * extended[0]
    pressure = PRESSURE_COEF * jnp.cumsum(density, axis=0)
    press_east = slope_x(pressure, mask_ext)
    press_north = slope_y(pressure, mask_ext)
    tendency = DIFFUSION * inner_lap - HYPERDIFF * second_lap - ADVECTION * (zonal * grad_east + merid * grad_north)
    nothing = jnp.zeros_like(zonal)
    forcing = jnp.stack([nothing, nothing, coriolis * merid - press_east, -coriolis * zonal - press_north])
    return mask_centre * (centre + (tendency + forcing))


def extend_global(existing_quantities, parity):
    top_rows = existing_quantities[:, :, MERIDIAN_POINTS - 2:, :][:, :, ::-1, ::-1] * parity[:, None, None, None]
    bottom = jnp.zeros(existing_quantities.shape[:2] + (2, existing_quantities.shape[3]), jnp.float32)
    extended = jnp.concatenate([bottom, existing_quantities, top_rows], axis=2)
    return jnp.concatenate([extended[..., -2:], extended, extended[..., :2]], axis=3)


def reference(thermal_deviation, saltiness_deviation, zonal_current_speed, meridional_flow_speed, water_indicator):
    wet_cells = water_indicator.astype(jnp.float32)[None]
    mask_ext = extend_global(wet_cells, jnp.ones((1,), jnp.float32))[0]
    parity = jnp.array([1.0, 1.0, -1.0, -1.0], jnp.float32)
    latitudes = jnp.arange(MERIDIAN_POINTS, dtype=jnp.int32).astype(jnp.float32)
    coriolis = (CORIOLIS_MAX * (2.0 * (latitudes + 0.5) / MERIDIAN_POINTS - 1.0))[:, None]
    existing_quantities = jnp.stack([thermal_deviation, saltiness_deviation, zonal_current_speed, meridional_flow_speed])
    for step_index in range(STEPS):
        existing_quantities = advance(extend_global(existing_quantities, parity), mask_ext, coriolis)
    return existing_quantities[0], existing_quantities[1], existing_quantities[2], existing_quantities[3]
```

```python
import functools

import jax
import jax.numpy as jnp
from jax import lax
from jax.experimental import pallas as pl
from jax.experimental.pallas import tpu as pltpu
from jax.sharding import PartitionSpec as P

STEPS = 4
HALO = 8

DIFFUSION = 0.1
HYPERDIFF = 0.01
ADVECTION = 0.25
EXPANSION = 0.2
CONTRACTION = 0.15
PRESSURE_COEF = 0.05
CORIOLIS_MAX = 0.3

MESH = pl.DeviceIdType.MESH
LANES = 128
SUB = 8


def lane_of(shape):
    return lax.broadcasted_iota(jnp.int32, shape, len(shape) - 1)


def take(x, idx):
    return jnp.take_along_axis(x, idx, axis=1)


def swap_bits(regs, lane):
    regs = list(regs)
    for k in range(3):
        dist = 16 << k
        low = (lane & dist) == 0
        for a in range(8):
            if a & (1 << k):
                continue
            b = a | (1 << k)
            x, y = regs[a], regs[b]
            regs[a] = jnp.where(low, x, pltpu.roll(y, dist, 1))
            regs[b] = jnp.where(low, pltpu.roll(x, LANES - dist, 1), y)
    return regs


def kernel(n_lon, n_lat, rows, t_in, s_in, u_in, v_in, m_in, t_out, s_out, u_out, v_out,
           raw, g, pm, lm, part, tot, coef, ax, ay, weak, cor,
           fold, send_w, send_e, recv_w, recv_e, ssem, rsem):
    lo = 2 * SUB
    hi = lo + rows
    blocks = rows // SUB
    half = rows // 2
    lon = lax.axis_index("lon")
    lat = lax.axis_index("lat")
    east = lax.rem(lon + 1, n_lon)
    west = lax.rem(lon + n_lon - 1, n_lon)
    mirror = n_lon - 1 - lon
    is_north = lat == n_lat - 1
    has_south = lat > 0
    north_lat = jnp.where(is_north, lat, lat + 1)
    north_lon = jnp.where(is_north, mirror, lon)
    ins = (t_in, s_in, u_in, v_in, m_in)
    outs = (t_out, s_out, u_out, v_out)

    barrier = pltpu.get_barrier_semaphore()
    for target in ((west, lat), (east, lat), (north_lon, north_lat)):
        pl.semaphore_signal(barrier, inc=1, device_id=target, device_id_type=MESH)

    @pl.when(has_south)
    def _():
        pl.semaphore_signal(barrier, inc=1, device_id=(lon, lat - 1), device_id_type=MESH)

    lane = lane_of((SUB, LANES))
    to_flat = 16 * (lane & 7) + (lane >> 3)
    to_cols = 8 * (lane & 15) + (lane >> 4)
    turned = 8 * (15 - (lane >> 3)) + (lane & 7)
    row8 = lax.broadcasted_iota(jnp.int32, (SUB, LANES), 0)

    def bring(b):
        r = pl.multiple_of(b * SUB, SUB)
        for a in range(5):
            regs = [ins[a][l, pl.ds(r, SUB), :] for l in range(8)]
            if a == 4:
                regs = [x.astype(jnp.float32) for x in regs]
            regs = swap_bits(regs, lane)
            for c in range(8):
                raw[a, c, pl.ds(lo + r, SUB), :] = take(regs[c], to_flat)

    def reverse_rows(x):
        for k in (4, 2, 1):
            up = pltpu.roll(x, SUB - k, 0)
            if k == 4:
                x = up
            else:
                x = jnp.where((row8 & k) == 0, up, pltpu.roll(x, k, 0))
        return x

    def fold_chunk(target, source):
        for a in range(5):
            x = raw[a, source, hi - SUB:hi, :]
            x = reverse_rows(take(x, turned))
            if a in (2, 3):
                x = -x
            fold[a, target] = x

    def copy(src, dst, k, target):
        return pltpu.make_async_remote_copy(
            src_ref=src, dst_ref=dst, send_sem=ssem.at[k], recv_sem=rsem.at[k],
            device_id=target, device_id_type=MESH)

    main = slice(0, 8)
    side = slice(8, 9)

    def to_north(part_slice, k):
        return copy(raw.at[:, part_slice, hi - SUB:hi], raw.at[:, part_slice, lo - SUB:lo],
                    k, (lon, lat + 1))

    def to_fold(part_slice, k):
        return copy(fold.at[:, part_slice], raw.at[:, part_slice, hi:hi + SUB],
                    k, (mirror, lat))

    def to_south(part_slice, k):
        return copy(raw.at[:, part_slice, lo:lo + SUB], raw.at[:, part_slice, hi:hi + SUB],
                    k, (lon, lat - 1))

    bring(blocks - 1)
    bring(0)

    @pl.when(is_north)
    def _():
        for c in range(8):
            fold_chunk(c, 7 - c)

    pl.semaphore_wait(barrier, jnp.where(has_south, 4, 3))

    def send_main():
        @pl.when(is_north)
        def _():
            to_fold(main, 0).start()

        @pl.when(jnp.logical_not(is_north))
        def _():
            to_north(main, 1).start()

        @pl.when(has_south)
        def _():
            to_south(main, 2).start()

    def send_side():
        @pl.when(is_north)
        def _():
            to_fold(side, 3).start()

        @pl.when(jnp.logical_not(is_north))
        def _():
            to_north(side, 4).start()

        @pl.when(has_south)
        def _():
            to_south(side, 5).start()

    send_main()

    @pl.loop(1, blocks - 1)
    def _(b):
        bring(b)

    near = lane_of((half, LANES)) < 64
    for a in range(5):
        first = raw[a, 0, lo:lo + half]
        second = raw[a, 0, lo + half:hi]
        send_w[a] = jnp.where(near, first, pltpu.roll(second, 64, 1))
        first = raw[a, 7, lo:lo + half]
        second = raw[a, 7, lo + half:hi]
        send_e[a] = jnp.where(near, pltpu.roll(first, 64, 1), second)
    go_w = copy(send_w, recv_e, 6, (west, lat))
    go_e = copy(send_e, recv_w, 7, (east, lat))
    go_w.start()
    go_e.start()

    nothing = jnp.zeros((9, SUB, LANES), jnp.float32)
    for ref in (raw, g, lm):
        for a in range(ref.shape[0]):
            ref[a, :, 0:SUB, :] = nothing
            ref[a, :, hi + SUB:hi + 2 * SUB, :] = nothing
    for r in (0, hi + SUB):
        pm[:, r:r + SUB, :] = nothing

    @pl.when(jnp.logical_not(has_south))
    def _():
        for a in range(5):
            raw[a, :, lo - SUB:lo, :] = nothing

    go_w.wait()
    go_e.wait()
    for a in range(5):
        x, y = recv_e[a], recv_w[a]
        raw[a, 8, lo:lo + half] = jnp.where(near, x, pltpu.roll(y, 64, 1))
        raw[a, 8, lo + half:hi] = jnp.where(near, pltpu.roll(x, 64, 1), y)

    @pl.when(is_north)
    def _():
        fold_chunk(8, 8)

    send_side()

    level = lane & 7
    scale = 0.5 * PRESSURE_COEF
    total = rows * n_lat

    def pressure(temperature, salinity):
        p = (scale * CONTRACTION) * salinity - (scale * EXPANSION) * temperature
        for k in (1, 2, 4):
            p = p + jnp.where(level >= k, pltpu.roll(p, k, 1), 0.0)
        return p

    def block(b):
        return pl.ds(pl.multiple_of(b * SUB, SUB), SUB)

    def columns(ref, lead, c, at):
        x = ref[(*lead, c, at, slice(None))]
        xe = ref[(*lead, (c + 1) % 9, at, slice(None))]
        xw = ref[(*lead, (c + 8) % 9, at, slice(None))]
        return (pltpu.roll(jnp.where(lane < 8, xe, x), LANES - 8, 1),
                pltpu.roll(jnp.where(lane >= LANES - 8, xw, x), 8, 1))

    def lines(ref, lead, c, b):
        return (ref[(*lead, c, pl.ds(b * SUB + 1, SUB), slice(None))],
                ref[(*lead, c, pl.ds(b * SUB - 1, SUB), slice(None))])

    def mask_state(b):
        at = block(b)
        for c in range(9):
            w = raw[4, c, at, :]
            pm[c, at, :] = w * pressure(raw[0, c, at, :], raw[1, c, at, :])
            for a in range(4):
                g[a, c, at, :] = w * raw[a, c, at, :]

    def constants(b):
        at = block(b)
        row = lat * rows + b * SUB - lo + row8
        row = jnp.where(row >= total, 2 * total - 1 - row, row).astype(jnp.float32)
        cor[at, :] = CORIOLIS_MAX * (2.0 * (row + 0.5) / total - 1.0)
        for c in range(9):
            w = raw[4, c, at, :]
            we, ww = columns(raw, (4,), c, at)
            wn, ws = lines(raw, (4,), c, b)
            s = (we + ww) + (wn + ws)
            tot[c, at, :] = s
            coef[c, at, :] = DIFFUSION + HYPERDIFF * s
            weak[c, at, :] = HYPERDIFF * w
            ax[c, at, :] = we - ww
            ay[c, at, :] = wn - ws

    def first_pass(b):
        at = block(b)
        f = cor[at, :]
        for c in range(9):
            w, s, k = raw[4, c, at, :], tot[c, at, :], coef[c, at, :]
            a_x, a_y = ax[c, at, :], ay[c, at, :]
            u, v = g[2, c, at, :], g[3, c, at, :]
            cu = (0.5 * ADVECTION) * u
            cv = (0.5 * ADVECTION) * v
            keep = 1.0 + (cu * a_x + cv * a_y)
            for a in range(4):
                x = g[a, c, at, :]
                xe, xw = columns(g, (a,), c, at)
                xn, xs = lines(g, (a,), c, b)
                lap = w * ((xe + xw) + (xn + xs)) - s * x
                lm[a, c, at, :] = lap
                new = keep * x - cu * (xe - xw) - cv * (xn - xs) + k * lap
                if a == 2:
                    pe, pw = columns(pm, (), c, at)
                    new = new + (f * v - w * (pe - pw) + a_x * pm[c, at, :])
                if a == 3:
                    pn, ps = lines(pm, (), c, b)
                    new = new - (f * u + w * (pn - ps) - a_y * pm[c, at, :])
                part[a, c, at, :] = new

    def second_pass(b, a, c):
        at = block(b)
        xe, xw = columns(lm, (a,), c, at)
        xn, xs = lines(lm, (a,), c, b)
        return part[a, c, at, :] - weak[c, at, :] * ((xe + xw) + (xn + xs))

    first_block = lo // SUB
    last_block = hi // SUB

    @pl.loop(first_block, last_block)
    def _(b):
        mask_state(b)

    @pl.loop(first_block + 1, last_block - 1)
    def _(b):
        constants(b)
        first_pass(b)

    @pl.when(is_north)
    def _():
        to_fold(main, 0).wait()
        to_fold(side, 3).wait()

    @pl.when(jnp.logical_not(is_north))
    def _():
        to_north(main, 1).wait_send()
        to_north(side, 4).wait_send()
        to_south(main, 2).wait_recv()
        to_south(side, 5).wait_recv()

    @pl.when(has_south)
    def _():
        to_south(main, 2).wait_send()
        to_south(side, 5).wait_send()
        to_north(main, 1).wait_recv()
        to_north(side, 4).wait_recv()

    mask_state(first_block - 1)
    mask_state(last_block)

    @pl.loop(0, 4)
    def _(k):
        b = jnp.where(k < 2, first_block - 1 + k, last_block - 3 + k)
        constants(b)
        first_pass(b)

    for step in range(STEPS):
        if step > 0:
            @pl.loop(first_block - 1, last_block + 1)
            def _(b):
                first_pass(b)

        if step < STEPS - 1:
            @pl.loop(first_block - 1, last_block + 1)
            def _(b):
                at = block(b)
                for c in range(9):
                    new = [second_pass(b, a, c) for a in range(4)]
                    pm[c, at, :] = raw[4, c, at, :] * pressure(new[0], new[1])
                    for a in range(4):
                        g[a, c, at, :] = new[a]
        else:
            @pl.loop(first_block, last_block)
            def _(b):
                at = pl.ds(pl.multiple_of((b - first_block) * SUB, SUB), SUB)
                for a in range(4):
                    regs = swap_bits([take(second_pass(b, a, c), to_cols) for c in range(8)], lane)
                    for l in range(8):
                        outs[a][l, at, :] = regs[l]


def shards(n_lon, n_lat, *fields):
    shape = fields[0].shape
    levels, rows, cols = shape
    assert levels == 8 and cols == LANES and rows % (2 * SUB) == 0 and rows >= 4 * SUB
    assert n_lon % 2 == 0 and n_lon > 2
    tall = rows + 4 * SUB
    vmem = pl.BlockSpec(memory_space=pltpu.VMEM)
    f32 = jnp.float32
    plane = pltpu.VMEM((9, tall, LANES), f32)
    state = pltpu.VMEM((4, 9, tall, LANES), f32)
    edge = pltpu.VMEM((5, rows // 2, LANES), f32)
    return tuple(pl.pallas_call(
        functools.partial(kernel, n_lon, n_lat, rows),
        out_shape=[jax.ShapeDtypeStruct(shape, f32)] * 4,
        in_specs=[vmem] * 5,
        out_specs=[vmem] * 4,
        scratch_shapes=[
            pltpu.VMEM((5, 9, tall, LANES), f32),
            state,
            plane,
            state,
            state,
            plane, plane, plane, plane, plane,
            pltpu.VMEM((tall, LANES), f32),
            pltpu.VMEM((5, 9, SUB, LANES), f32),
            edge, edge, edge, edge,
            pltpu.SemaphoreType.DMA((8,)),
            pltpu.SemaphoreType.DMA((8,)),
        ],
        compiler_params=pltpu.CompilerParams(
            collective_id=0, has_side_effects=True, vmem_limit_bytes=40 * 1024 * 1024),
    )(*fields))


def solution(mesh):
    placed = P(None, "lat", "lon")
    return jax.shard_map(
        functools.partial(shards, mesh.shape["lon"], mesh.shape["lat"]),
        mesh=mesh,
        in_specs=(placed,) * 5,
        out_specs=(placed,) * 4,
        check_vma=False,
    )
```

```python
import functools

import jax
import jax.numpy as jnp
from jax import lax
from jax.experimental import pallas as pl
from jax.experimental.pallas import tpu as pltpu
from jax.sharding import PartitionSpec as P

STEPS = 4
HALO = 8

DIFFUSION = 0.1
HYPERDIFF = 0.01
ADVECTION = 0.25
EXPANSION = 0.2
CONTRACTION = 0.15
PRESSURE_COEF = 0.05
CORIOLIS_MAX = 0.3

MESH = pl.DeviceIdType.MESH
LANES = 128
SUB = 8


def lane_of(shape):
    return lax.broadcasted_iota(jnp.int32, shape, len(shape) - 1)


def take(x, idx):
    return jnp.take_along_axis(x, idx, axis=1)


def swap_bits(regs, lane):
    regs = list(regs)
    for k in range(3):
        dist = 1 << k
        low = (lane & dist) == 0
        for a in range(8):
            if a & (1 << k):
                continue
            b = a | (1 << k)
            x, y = regs[a], regs[b]
            regs[a] = jnp.where(low, x, pltpu.roll(y, dist, 1))
            regs[b] = jnp.where(low, pltpu.roll(x, LANES - dist, 1), y)
    return regs


def kernel(n_lon, n_lat, rows, t_hbm, s_hbm, u_hbm, v_hbm, m_hbm, t_out, s_out, u_out, v_out,
           raw, g, pm, lm, part, tot, coef, ax, ay, weak, cor,
           fold, send_w, send_e, recv_w, recv_e, t_in, s_in, u_in, v_in, m_in,
           ssem, rsem, isem):
    lo = 2 * SUB
    hi = lo + rows
    blocks = rows // SUB
    half = rows // 2
    lon = lax.axis_index("lon")
    lat = lax.axis_index("lat")
    east = lax.rem(lon + 1, n_lon)
    west = lax.rem(lon + n_lon - 1, n_lon)
    mirror = n_lon - 1 - lon
    is_north = lat == n_lat - 1
    has_south = lat > 0
    north_lat = jnp.where(is_north, lat, lat + 1)
    north_lon = jnp.where(is_north, mirror, lon)
    ins = (t_in, s_in, u_in, v_in, m_in)
    outs = (t_out, s_out, u_out, v_out)
    loads = [pltpu.make_async_copy(src, dst, isem.at[k])
             for k, (src, dst) in enumerate(zip((t_hbm, s_hbm, u_hbm, v_hbm, m_hbm), ins))]
    for load in loads:
        load.start()

    barrier = pltpu.get_barrier_semaphore()
    for target in ((west, lat), (east, lat), (north_lon, north_lat)):
        pl.semaphore_signal(barrier, inc=1, device_id=target, device_id_type=MESH)

    @pl.when(has_south)
    def _():
        pl.semaphore_signal(barrier, inc=1, device_id=(lon, lat - 1), device_id_type=MESH)

    lane = lane_of((SUB, LANES))
    rims = jnp.where(lane < 64, 0, LANES - 8) + (lane & 7)
    turned = 8 * (15 - (lane >> 3)) + (lane & 7)
    row8 = lax.broadcasted_iota(jnp.int32, (SUB, LANES), 0)

    def bring(b):
        r = pl.multiple_of(b * SUB, SUB)
        for a in range(5):
            regs = [ins[a][l, pl.ds(r, SUB), :] for l in range(8)]
            if a == 4:
                regs = [x.astype(jnp.float32) for x in regs]
            regs = swap_bits(regs, lane)
            for c in range(8):
                raw[a, c, pl.ds(lo + r, SUB), :] = regs[c]
            rim = take(regs[0], rims)
            for c in range(1, 8):
                rim = jnp.where(((lane >> 3) & 7) == c, take(regs[c], rims), rim)
            raw[a, 8, pl.ds(lo + r, SUB), :] = rim

    def reverse_rows(x):
        for k in (4, 2, 1):
            up = pltpu.roll(x, SUB - k, 0)
            if k == 4:
                x = up
            else:
                x = jnp.where((row8 & k) == 0, up, pltpu.roll(x, k, 0))
        return x

    def fold_chunk(target, source):
        for a in range(5):
            x = raw[a, source, hi - SUB:hi, :]
            x = reverse_rows(take(x, turned))
            if a in (2, 3):
                x = -x
            fold[a, target] = x

    def copy(src, dst, k, target):
        return pltpu.make_async_remote_copy(
            src_ref=src, dst_ref=dst, send_sem=ssem.at[k], recv_sem=rsem.at[k],
            device_id=target, device_id_type=MESH)

    main = slice(0, 8)
    side = slice(8, 9)

    def to_north(part_slice, k):
        return copy(raw.at[:, part_slice, hi - SUB:hi], raw.at[:, part_slice, lo - SUB:lo],
                    k, (lon, lat + 1))

    def to_fold(part_slice, k):
        return copy(fold.at[:, part_slice], raw.at[:, part_slice, hi:hi + SUB],
                    k, (mirror, lat))

    def to_south(part_slice, k):
        return copy(raw.at[:, part_slice, lo:lo + SUB], raw.at[:, part_slice, hi:hi + SUB],
                    k, (lon, lat - 1))

    for load in loads:
        load.wait()
    bring(blocks - 1)
    bring(0)

    @pl.when(is_north)
    def _():
        for c in range(8):
            fold_chunk(c, 7 - c)

    pl.semaphore_wait(barrier, jnp.where(has_south, 4, 3))

    def send_main():
        @pl.when(is_north)
        def _():
            to_fold(main, 0).start()

        @pl.when(jnp.logical_not(is_north))
        def _():
            to_north(main, 1).start()

        @pl.when(has_south)
        def _():
            to_south(main, 2).start()

    def send_side():
        @pl.when(is_north)
        def _():
            to_fold(side, 3).start()

        @pl.when(jnp.logical_not(is_north))
        def _():
            to_north(side, 4).start()

        @pl.when(has_south)
        def _():
            to_south(side, 5).start()

    send_main()

    @pl.loop(1, blocks - 1)
    def _(b):
        bring(b)

    near = lane_of((half, LANES)) < 64
    for a in range(5):
        first = raw[a, 8, lo:lo + half]
        second = raw[a, 8, lo + half:hi]
        send_w[a] = jnp.where(near, first, pltpu.roll(second, 64, 1))
        first = raw[a, 8, lo:lo + half]
        second = raw[a, 8, lo + half:hi]
        send_e[a] = jnp.where(near, pltpu.roll(first, 64, 1), second)
    go_w = copy(send_w, recv_e, 6, (west, lat))
    go_e = copy(send_e, recv_w, 7, (east, lat))
    go_w.start()
    go_e.start()

    nothing = jnp.zeros((9, SUB, LANES), jnp.float32)
    for ref in (raw, g, lm):
        for a in range(ref.shape[0]):
            ref[a, :, 0:SUB, :] = nothing
            ref[a, :, hi + SUB:hi + 2 * SUB, :] = nothing
    for r in (0, hi + SUB):
        pm[:, r:r + SUB, :] = nothing

    @pl.when(jnp.logical_not(has_south))
    def _():
        for a in range(5):
            raw[a, :, lo - SUB:lo, :] = nothing

    go_w.wait()
    go_e.wait()
    for a in range(5):
        x, y = recv_e[a], recv_w[a]
        raw[a, 8, lo:lo + half] = jnp.where(near, x, pltpu.roll(y, 64, 1))
        raw[a, 8, lo + half:hi] = jnp.where(near, pltpu.roll(x, 64, 1), y)

    @pl.when(is_north)
    def _():
        fold_chunk(8, 8)

    send_side()

    level = lane & 7
    scale = 0.5 * PRESSURE_COEF
    total = rows * n_lat

    def pressure(temperature, salinity):
        p = (scale * CONTRACTION) * salinity - (scale * EXPANSION) * temperature
        for k in (1, 2, 4):
            p = p + jnp.where(level >= k, pltpu.roll(p, k, 1), 0.0)
        return p

    def block(b):
        return pl.ds(pl.multiple_of(b * SUB, SUB), SUB)

    def columns(ref, lead, c, at):
        def get(i):
            return ref[(*lead, i, at, slice(None))]

        if c < 7:
            xe = get(c + 1)
        else:
            far, near_by = (8, 0) if c == 7 else (0, 8)
            xe = pltpu.roll(jnp.where(lane < 8, get(far), get(near_by)), LANES - 8, 1)
        if 0 < c < 8:
            xw = get(c - 1)
        else:
            far, near_by = (8, 7) if c == 0 else (7, 8)
            xw = pltpu.roll(jnp.where(lane >= LANES - 8, get(far), get(near_by)), 8, 1)
        return xe, xw

    def lines(ref, lead, c, b):
        return (ref[(*lead, c, pl.ds(b * SUB + 1, SUB), slice(None))],
                ref[(*lead, c, pl.ds(b * SUB - 1, SUB), slice(None))])

    def mask_state(b):
        at = block(b)
        for c in range(9):
            w = raw[4, c, at, :]
            pm[c, at, :] = w * pressure(raw[0, c, at, :], raw[1, c, at, :])
            for a in range(4):
                g[a, c, at, :] = w * raw[a, c, at, :]

    def constants(b):
        at = block(b)
        row = lat * rows + b * SUB - lo + row8
        row = jnp.where(row >= total, 2 * total - 1 - row, row).astype(jnp.float32)
        cor[at, :] = CORIOLIS_MAX * (2.0 * (row + 0.5) / total - 1.0)
        for c in range(9):
            w = raw[4, c, at, :]
            we, ww = columns(raw, (4,), c, at)
            wn, ws = lines(raw, (4,), c, b)
            s = (we + ww) + (wn + ws)
            tot[c, at, :] = s
            coef[c, at, :] = DIFFUSION + HYPERDIFF * s
            weak[c, at, :] = HYPERDIFF * w
            ax[c, at, :] = we - ww
            ay[c, at, :] = wn - ws

    def first_pass(b):
        at = block(b)
        f = cor[at, :]
        for c in range(9):
            w, s, k = raw[4, c, at, :], tot[c, at, :], coef[c, at, :]
            a_x, a_y = ax[c, at, :], ay[c, at, :]
            u, v = g[2, c, at, :], g[3, c, at, :]
            cu = (0.5 * ADVECTION) * u
            cv = (0.5 * ADVECTION) * v
            keep = 1.0 + (cu * a_x + cv * a_y)
            for a in range(4):
                x = g[a, c, at, :]
                xe, xw = columns(g, (a,), c, at)
                xn, xs = lines(g, (a,), c, b)
                lap = w * ((xe + xw) + (xn + xs)) - s * x
                lm[a, c, at, :] = lap
                new = keep * x - cu * (xe - xw) - cv * (xn - xs) + k * lap
                if a == 2:
                    pe, pw = columns(pm, (), c, at)
                    new = new + (f * v - w * (pe - pw) + a_x * pm[c, at, :])
                if a == 3:
                    pn, ps = lines(pm, (), c, b)
                    new = new - (f * u + w * (pn - ps) - a_y * pm[c, at, :])
                part[a, c, at, :] = new

    def second_pass(b, a, c):
        at = block(b)
        xe, xw = columns(lm, (a,), c, at)
        xn, xs = lines(lm, (a,), c, b)
        return part[a, c, at, :] - weak[c, at, :] * ((xe + xw) + (xn + xs))

    first_block = lo // SUB
    last_block = hi // SUB

    @pl.loop(first_block, last_block)
    def _(b):
        mask_state(b)

    @pl.loop(first_block + 1, last_block - 1)
    def _(b):
        constants(b)
        first_pass(b)

    @pl.when(is_north)
    def _():
        to_fold(main, 0).wait()
        to_fold(side, 3).wait()

    @pl.when(jnp.logical_not(is_north))
    def _():
        to_north(main, 1).wait_send()
        to_north(side, 4).wait_send()
        to_south(main, 2).wait_recv()
        to_south(side, 5).wait_recv()

    @pl.when(has_south)
    def _():
        to_south(main, 2).wait_send()
        to_south(side, 5).wait_send()
        to_north(main, 1).wait_recv()
        to_north(side, 4).wait_recv()

    mask_state(first_block - 1)
    mask_state(last_block)

    @pl.loop(0, 4)
    def _(k):
        b = jnp.where(k < 2, first_block - 1 + k, last_block - 3 + k)
        constants(b)
        first_pass(b)

    for step in range(STEPS):
        if step > 0:
            @pl.loop(first_block - 1, last_block + 1)
            def _(b):
                first_pass(b)

        if step < STEPS - 1:
            @pl.loop(first_block - 1, last_block + 1)
            def _(b):
                at = block(b)
                for c in range(9):
                    new = [second_pass(b, a, c) for a in range(4)]
                    pm[c, at, :] = raw[4, c, at, :] * pressure(new[0], new[1])
                    for a in range(4):
                        g[a, c, at, :] = new[a]
        else:
            @pl.loop(first_block, last_block)
            def _(b):
                at = pl.ds(pl.multiple_of((b - first_block) * SUB, SUB), SUB)
                for a in range(4):
                    regs = swap_bits([second_pass(b, a, c) for c in range(8)], lane)
                    for l in range(8):
                        outs[a][l, at, :] = regs[l]


def shards(n_lon, n_lat, *fields):
    shape = fields[0].shape
    levels, rows, cols = shape
    assert levels == 8 and cols == LANES and rows % (2 * SUB) == 0 and rows >= 4 * SUB
    assert n_lon % 2 == 0 and n_lon > 2
    tall = rows + 4 * SUB
    vmem = pl.BlockSpec(memory_space=pltpu.VMEM)
    f32 = jnp.float32
    plane = pltpu.VMEM((9, tall, LANES), f32)
    state = pltpu.VMEM((4, 9, tall, LANES), f32)
    edge = pltpu.VMEM((5, rows // 2, LANES), f32)
    new = pl.pallas_call(
        functools.partial(kernel, n_lon, n_lat, rows),
        out_shape=[jax.ShapeDtypeStruct(shape, f32)] * 4,
        in_specs=[pl.BlockSpec(memory_space=pltpu.HBM)] * 5,
        out_specs=[vmem] * 4,
        scratch_shapes=[
            pltpu.VMEM((5, 9, tall, LANES), f32),
            state,
            plane,
            state,
            state,
            plane, plane, plane, plane, plane,
            pltpu.VMEM((tall, LANES), f32),
            pltpu.VMEM((5, 9, SUB, LANES), f32),
            edge, edge, edge, edge,
            *[pltpu.VMEM(shape, x.dtype) for x in fields],
            pltpu.SemaphoreType.DMA((8,)),
            pltpu.SemaphoreType.DMA((8,)),
            pltpu.SemaphoreType.DMA((5,)),
        ],
        compiler_params=pltpu.CompilerParams(
            collective_id=0, has_side_effects=True, vmem_limit_bytes=(64 * 1024 - 1024 - 128) * 1024),
    )(*fields)
    water = fields[4] != 0
    return tuple(jnp.where(water, x, 0.0) for x in new)


def solution(mesh):
    placed = P(None, "lat", "lon")
    return jax.shard_map(
        functools.partial(shards, mesh.shape["lon"], mesh.shape["lat"]),
        mesh=mesh,
        in_specs=(placed,) * 5,
        out_specs=(placed,) * 4,
        check_vma=False,
    )
```

```python
import functools

import jax
import jax.numpy as jnp
from jax import lax
from jax.experimental import pallas as pl
from jax.experimental.pallas import tpu as pltpu
from jax.sharding import PartitionSpec as P

STEPS = 4
HALO = 8

DIFFUSION = 0.1
HYPERDIFF = 0.01
ADVECTION = 0.25
EXPANSION = 0.2
CONTRACTION = 0.15
PRESSURE_COEF = 0.05
CORIOLIS_MAX = 0.3

MESH = pl.DeviceIdType.MESH
LANES = 128
SUB = 8


def lane_of(shape):
    return lax.broadcasted_iota(jnp.int32, shape, len(shape) - 1)


def take(x, idx):
    return jnp.take_along_axis(x, idx, axis=1)


def swap_bits(regs, lane):
    regs = list(regs)
    for k in range(3):
        dist = 1 << k
        low = (lane & dist) == 0
        for a in range(8):
            if a & (1 << k):
                continue
            b = a | (1 << k)
            x, y = regs[a], regs[b]
            regs[a] = jnp.where(low, x, pltpu.roll(y, dist, 1))
            regs[b] = jnp.where(low, pltpu.roll(x, LANES - dist, 1), y)
    return regs


def kernel(n_lon, n_lat, rows, t_hbm, s_hbm, u_hbm, v_hbm, m_hbm, t_out, s_out, u_out, v_out,
           raw, g, pm, lm, part, tot, coef, ax, ay, weak, cor,
           fold, send_w, send_e, recv_w, recv_e, t_in, s_in, u_in, v_in, m_in,
           ssem, rsem, isem):
    lo = 2 * SUB
    hi = lo + rows
    blocks = rows // SUB
    half = rows // 2
    lon = lax.axis_index("lon")
    lat = lax.axis_index("lat")
    east = lax.rem(lon + 1, n_lon)
    west = lax.rem(lon + n_lon - 1, n_lon)
    mirror = n_lon - 1 - lon
    is_north = lat == n_lat - 1
    has_south = lat > 0
    north_lat = jnp.where(is_north, lat, lat + 1)
    north_lon = jnp.where(is_north, mirror, lon)
    ins = (t_in, s_in, u_in, v_in, m_in)
    outs = (t_out, s_out, u_out, v_out)
    loads = [pltpu.make_async_copy(src, dst, isem.at[k])
             for k, (src, dst) in enumerate(zip((t_hbm, s_hbm, u_hbm, v_hbm, m_hbm), ins))]
    for load in loads:
        load.start()

    barrier = pltpu.get_barrier_semaphore()
    for target in ((west, lat), (east, lat), (north_lon, north_lat)):
        pl.semaphore_signal(barrier, inc=1, device_id=target, device_id_type=MESH)

    @pl.when(has_south)
    def _():
        pl.semaphore_signal(barrier, inc=1, device_id=(lon, lat - 1), device_id_type=MESH)

    lane = lane_of((SUB, LANES))
    rims = jnp.where(lane < 64, 0, LANES - 8) + (lane & 7)
    turned = 8 * (15 - (lane >> 3)) + (lane & 7)
    row8 = lax.broadcasted_iota(jnp.int32, (SUB, LANES), 0)

    def bring(b):
        r = pl.multiple_of(b * SUB, SUB)
        for a in range(5):
            regs = [ins[a][l, pl.ds(r, SUB), :] for l in range(8)]
            if a == 4:
                regs = [x.astype(jnp.float32) for x in regs]
            regs = swap_bits(regs, lane)
            for c in range(8):
                raw[a, c, pl.ds(lo + r, SUB), :] = regs[c]
            rim = take(regs[0], rims)
            for c in range(1, 8):
                rim = jnp.where(((lane >> 3) & 7) == c, take(regs[c], rims), rim)
            raw[a, 8, pl.ds(lo + r, SUB), :] = rim

    def reverse_rows(x):
        for k in (4, 2, 1):
            up = pltpu.roll(x, SUB - k, 0)
            if k == 4:
                x = up
            else:
                x = jnp.where((row8 & k) == 0, up, pltpu.roll(x, k, 0))
        return x

    def fold_chunk(target, source):
        for a in range(5):
            x = raw[a, source, hi - SUB:hi, :]
            x = reverse_rows(take(x, turned))
            if a in (2, 3):
                x = -x
            fold[a, target] = x

    def copy(src, dst, k, target):
        return pltpu.make_async_remote_copy(
            src_ref=src, dst_ref=dst, send_sem=ssem.at[k], recv_sem=rsem.at[k],
            device_id=target, device_id_type=MESH)

    main = slice(0, 8)
    side = slice(8, 9)

    def to_north(part_slice, k):
        return copy(raw.at[:, part_slice, hi - SUB:hi], raw.at[:, part_slice, lo - SUB:lo],
                    k, (lon, lat + 1))

    def to_fold(part_slice, k):
        return copy(fold.at[:, part_slice], raw.at[:, part_slice, hi:hi + SUB],
                    k, (mirror, lat))

    def to_south(part_slice, k):
        return copy(raw.at[:, part_slice, lo:lo + SUB], raw.at[:, part_slice, hi:hi + SUB],
                    k, (lon, lat - 1))

    for load in loads:
        load.wait()
    bring(blocks - 1)
    bring(0)

    @pl.when(is_north)
    def _():
        for c in range(8):
            fold_chunk(c, 7 - c)

    pl.semaphore_wait(barrier, jnp.where(has_south, 4, 3))

    def send_main():
        @pl.when(is_north)
        def _():
            to_fold(main, 0).start()

        @pl.when(jnp.logical_not(is_north))
        def _():
            to_north(main, 1).start()

        @pl.when(has_south)
        def _():
            to_south(main, 2).start()

    def send_side():
        @pl.when(is_north)
        def _():
            to_fold(side, 3).start()

        @pl.when(jnp.logical_not(is_north))
        def _():
            to_north(side, 4).start()

        @pl.when(has_south)
        def _():
            to_south(side, 5).start()

    send_main()

    @pl.loop(1, blocks - 1)
    def _(b):
        bring(b)

    near = lane_of((half, LANES)) < 64
    for a in range(5):
        first = raw[a, 8, lo:lo + half]
        second = raw[a, 8, lo + half:hi]
        send_w[a] = jnp.where(near, first, pltpu.roll(second, 64, 1))
        first = raw[a, 8, lo:lo + half]
        second = raw[a, 8, lo + half:hi]
        send_e[a] = jnp.where(near, pltpu.roll(first, 64, 1), second)
    go_w = copy(send_w, recv_e, 6, (west, lat))
    go_e = copy(send_e, recv_w, 7, (east, lat))
    go_w.start()
    go_e.start()

    nothing = jnp.zeros((9, SUB, LANES), jnp.float32)
    for ref in (raw, g, lm):
        for a in range(ref.shape[0]):
            ref[a, :, 0:SUB, :] = nothing
            ref[a, :, hi + SUB:hi + 2 * SUB, :] = nothing
    for r in (0, hi + SUB):
        pm[:, r:r + SUB, :] = nothing

    @pl.when(jnp.logical_not(has_south))
    def _():
        for a in range(5):
            raw[a, :, lo - SUB:lo, :] = nothing

    level = lane & 7
    scale = 0.5 * PRESSURE_COEF
    total = rows * n_lat

    def pressure(temperature, salinity):
        p = (scale * CONTRACTION) * salinity - (scale * EXPANSION) * temperature
        for k in (1, 2, 4):
            p = p + jnp.where(level >= k, pltpu.roll(p, k, 1), 0.0)
        return p

    def block(b):
        return pl.ds(pl.multiple_of(b * SUB, SUB), SUB)

    def columns(ref, lead, c, at):
        def get(i):
            return ref[(*lead, i, at, slice(None))]

        if c < 7:
            xe = get(c + 1)
        else:
            far, near_by = (8, 0) if c == 7 else (0, 8)
            xe = pltpu.roll(jnp.where(lane < 8, get(far), get(near_by)), LANES - 8, 1)
        if 0 < c < 8:
            xw = get(c - 1)
        else:
            far, near_by = (8, 7) if c == 0 else (7, 8)
            xw = pltpu.roll(jnp.where(lane >= LANES - 8, get(far), get(near_by)), 8, 1)
        return xe, xw

    def lines(ref, lead, c, b):
        return (ref[(*lead, c, pl.ds(b * SUB + 1, SUB), slice(None))],
                ref[(*lead, c, pl.ds(b * SUB - 1, SUB), slice(None))])

    def mask_state(b, chunks=range(9)):
        at = block(b)
        for c in chunks:
            w = raw[4, c, at, :]
            pm[c, at, :] = w * pressure(raw[0, c, at, :], raw[1, c, at, :])
            for a in range(4):
                g[a, c, at, :] = w * raw[a, c, at, :]

    def constants(b, chunks=range(9)):
        at = block(b)
        row = lat * rows + b * SUB - lo + row8
        row = jnp.where(row >= total, 2 * total - 1 - row, row).astype(jnp.float32)
        cor[at, :] = CORIOLIS_MAX * (2.0 * (row + 0.5) / total - 1.0)
        for c in chunks:
            w = raw[4, c, at, :]
            we, ww = columns(raw, (4,), c, at)
            wn, ws = lines(raw, (4,), c, b)
            s = (we + ww) + (wn + ws)
            tot[c, at, :] = s
            coef[c, at, :] = DIFFUSION + HYPERDIFF * s
            weak[c, at, :] = HYPERDIFF * w
            ax[c, at, :] = we - ww
            ay[c, at, :] = wn - ws

    def first_pass(b, chunks=range(9)):
        at = block(b)
        f = cor[at, :]
        for c in chunks:
            w, s, k = raw[4, c, at, :], tot[c, at, :], coef[c, at, :]
            a_x, a_y = ax[c, at, :], ay[c, at, :]
            u, v = g[2, c, at, :], g[3, c, at, :]
            cu = (0.5 * ADVECTION) * u
            cv = (0.5 * ADVECTION) * v
            keep = 1.0 + (cu * a_x + cv * a_y)
            for a in range(4):
                x = g[a, c, at, :]
                xe, xw = columns(g, (a,), c, at)
                xn, xs = lines(g, (a,), c, b)
                lap = w * ((xe + xw) + (xn + xs)) - s * x
                lm[a, c, at, :] = lap
                new = keep * x - cu * (xe - xw) - cv * (xn - xs) + k * lap
                if a == 2:
                    pe, pw = columns(pm, (), c, at)
                    new = new + (f * v - w * (pe - pw) + a_x * pm[c, at, :])
                if a == 3:
                    pn, ps = lines(pm, (), c, b)
                    new = new - (f * u + w * (pn - ps) - a_y * pm[c, at, :])
                part[a, c, at, :] = new

    def second_pass(b, a, c):
        at = block(b)
        xe, xw = columns(lm, (a,), c, at)
        xn, xs = lines(lm, (a,), c, b)
        return part[a, c, at, :] - weak[c, at, :] * ((xe + xw) + (xn + xs))

    first_block = lo // SUB
    last_block = hi // SUB

    @pl.loop(first_block, last_block)
    def _(b):
        mask_state(b, range(8))

    @pl.loop(first_block + 1, last_block - 1)
    def _(b):
        constants(b, range(1, 7))
        first_pass(b, range(1, 7))

    go_w.wait()
    go_e.wait()
    for a in range(5):
        x, y = recv_e[a], recv_w[a]
        raw[a, 8, lo:lo + half] = jnp.where(near, x, pltpu.roll(y, 64, 1))
        raw[a, 8, lo + half:hi] = jnp.where(near, pltpu.roll(x, 64, 1), y)

    @pl.when(is_north)
    def _():
        fold_chunk(8, 8)

    send_side()

    @pl.loop(first_block, last_block)
    def _(b):
        mask_state(b, (8,))

    @pl.loop(first_block + 1, last_block - 1)
    def _(b):
        constants(b, (7, 8, 0))
        first_pass(b, (7, 8, 0))

    @pl.when(is_north)
    def _():
        to_fold(main, 0).wait()
        to_fold(side, 3).wait()

    @pl.when(jnp.logical_not(is_north))
    def _():
        to_north(main, 1).wait_send()
        to_north(side, 4).wait_send()
        to_south(main, 2).wait_recv()
        to_south(side, 5).wait_recv()

    @pl.when(has_south)
    def _():
        to_south(main, 2).wait_send()
        to_south(side, 5).wait_send()
        to_north(main, 1).wait_recv()
        to_north(side, 4).wait_recv()

    mask_state(first_block - 1)
    mask_state(last_block)

    @pl.loop(0, 4)
    def _(k):
        b = jnp.where(k < 2, first_block - 1 + k, last_block - 3 + k)
        constants(b)
        first_pass(b)

    for step in range(STEPS):
        if step > 0:
            @pl.loop(first_block - 1, last_block + 1, unroll=2)
            def _(b):
                first_pass(b)

        if step < STEPS - 1:
            @pl.loop(first_block - 1, last_block + 1, unroll=2)
            def _(b):
                at = block(b)
                for c in range(9):
                    new = [second_pass(b, a, c) for a in range(4)]
                    pm[c, at, :] = raw[4, c, at, :] * pressure(new[0], new[1])
                    for a in range(4):
                        g[a, c, at, :] = new[a]
        else:
            @pl.loop(first_block, last_block)
            def _(b):
                at = pl.ds(pl.multiple_of((b - first_block) * SUB, SUB), SUB)
                for a in range(4):
                    regs = swap_bits([second_pass(b, a, c) for c in range(8)], lane)
                    for l in range(8):
                        outs[a][l, at, :] = regs[l]


def shards(n_lon, n_lat, *fields):
    shape = fields[0].shape
    levels, rows, cols = shape
    assert levels == 8 and cols == LANES and rows % (2 * SUB) == 0 and rows >= 4 * SUB
    assert n_lon % 2 == 0 and n_lon > 2
    tall = rows + 4 * SUB
    vmem = pl.BlockSpec(memory_space=pltpu.VMEM)
    f32 = jnp.float32
    plane = pltpu.VMEM((9, tall, LANES), f32)
    state = pltpu.VMEM((4, 9, tall, LANES), f32)
    edge = pltpu.VMEM((5, rows // 2, LANES), f32)
    new = pl.pallas_call(
        functools.partial(kernel, n_lon, n_lat, rows),
        out_shape=[jax.ShapeDtypeStruct(shape, f32)] * 4,
        in_specs=[pl.BlockSpec(memory_space=pltpu.HBM)] * 5,
        out_specs=[vmem] * 4,
        scratch_shapes=[
            pltpu.VMEM((5, 9, tall, LANES), f32),
            state,
            plane,
            state,
            state,
            plane, plane, plane, plane, plane,
            pltpu.VMEM((tall, LANES), f32),
            pltpu.VMEM((5, 9, SUB, LANES), f32),
            edge, edge, edge, edge,
            *[pltpu.VMEM(shape, x.dtype) for x in fields],
            pltpu.SemaphoreType.DMA((8,)),
            pltpu.SemaphoreType.DMA((8,)),
            pltpu.SemaphoreType.DMA((5,)),
        ],
        compiler_params=pltpu.CompilerParams(
            collective_id=0, has_side_effects=True, vmem_limit_bytes=(64 * 1024 - 1024 - 128) * 1024),
    )(*fields)
    water = fields[4] != 0
    return tuple(jnp.where(water, x, 0.0) for x in new)


def solution(mesh):
    placed = P(None, "lat", "lon")
    return jax.shard_map(
        functools.partial(shards, mesh.shape["lon"], mesh.shape["lat"]),
        mesh=mesh,
        in_specs=(placed,) * 5,
        out_specs=(placed,) * 4,
        check_vma=False,
    )
```
